32 devices in a mesh: gx: 8 (over z, x), gy: 2 (over core), gz: 2 (over y).
Axes of the slice: x: 2, y: 2, z: 4, core: 2. Of those that a mesh axis runs over, the one named last changes fastest.
Arguments:
- bands: float32 [4, 96, 96, 256], P(None, 'gx', 'gy', 'gz'), may hold values from -6 to 6
- stencil_coef: float32 [27], replicated, may hold values from -0.12 to 0.12
Outputs:
- basis: float32 [4, 96, 96, 256], P(None, 'gx', 'gy', 'gz')
- ritz: float32 [4, 4], replicated
The draws below stay inside these ranges and needn't reach their ends.
All inputs are finite; a program needn't handle non-finite values.
Results may differ from the reference program's by a relative error of at most 0.000071.
Values sent between devices are 32-bit elements; how exact they have to be, the bound alone decides.
A program may use at most 64 MiB of HBM per device.

```python
import jax
import jax.numpy as jnp
from jax import lax

NB = 4
DEGREE = 4
NX = 96
NY = 96
NZ = 256
NCELLS = 2359296


def levels(key, dims, split, smallest, high):
    def one(dim, blocks):
        draws = jax.random.uniform(jax.random.fold_in(jax.random.fold_in(key, 6), dim), (blocks,), jnp.float32, smallest / len(split), high / len(split))
        return jnp.repeat(jnp.exp(draws), dims[dim] // blocks).reshape((-1,) + (1,) * (len(dims) - dim - 1))

    loudness = one(*split[0])
    for cut in split[1:]:
        loudness = loudness * one(*cut)
    return loudness


def bell_draw(rng, dims, scale, most, cuts=(), kind=jnp.bfloat16):
    values = scale * jax.random.normal(rng, dims, jnp.float32)
    if cuts:
        values = values * levels(rng, dims, cuts, -0.22, 0.18)
    return jnp.clip(values, -most, most).astype(kind)


def setup_inputs(seed: int = 0) -> dict:
    key_list = jax.random.split(jax.random.key(seed), 3)
    return {
        "bands": bell_draw(key_list[0], (NB, NX, NY, NZ), 1.0, 6.0, ((1, 8), (2, 2), (3, 2)), jnp.float32),
        "stencil_coef": jnp.clip(jax.random.uniform(key_list[1], (27,), jnp.float32, -0.12, 0.12), -0.12, 0.12),
    }


lower_edge = 1.0
upper_edge = 6.5

def axis_squares(total):
    position = jnp.arange(total, dtype=jnp.int32)
    scaled = jnp.minimum(position, total - position).astype(jnp.float32) / (0.5 * total)
    return scaled * scaled

def apply_band(field, kinetic, coefficients):
    result = kinetic * field
    position = 0
    for shift_x in (-1, 0, 1):
        for shift_y in (-1, 0, 1):
            for shift_z in (-1, 0, 1):
                moved = jnp.roll(field, (-shift_x, -shift_y, -shift_z), (0, 1, 2))
                result = result + coefficients[position] * moved
                position += 1
    return result

def apply_all(field, kinetic, coefficients):
    return jnp.stack([apply_band(field[band], kinetic, coefficients) for band in range(NB)])

def reference(bands, stencil_coef):
    square_x = axis_squares(NX)
    square_y = axis_squares(NY)
    square_z = axis_squares(NZ)
    kinetic = square_x[:, None, None] + square_y[None, :, None] + square_z[None, None, :]
    half = (upper_edge - lower_edge) / 2
    center = (upper_edge + lower_edge) / 2
    previous = bands
    current = (apply_all(bands, kinetic, stencil_coef) - center * bands) / half
    for degree in range(1, DEGREE):
        following = 2.0 * (apply_all(current, kinetic, stencil_coef) - center * current) / half - previous
        previous = current
        current = following
    flattened = current.reshape(NB, -1)
    gram = jnp.dot(flattened, flattened.T, precision=lax.Precision.HIGHEST) / NCELLS
    lower_factor = jnp.linalg.cholesky(gram)
    inverse = jax.scipy.linalg.solve_triangular(lower_factor, jnp.eye(NB, dtype=jnp.float32), lower=True)
    basis_flat = jnp.dot(inverse, flattened, precision=lax.Precision.HIGHEST)
    basis = basis_flat.reshape(current.shape)
    image = apply_all(basis, kinetic, stencil_coef).reshape(NB, -1)
    projected = jnp.dot(basis_flat, image.T, precision=lax.Precision.HIGHEST) / NCELLS
    return (basis, projected)
```

```python
import functools

import jax
import jax.numpy as jnp
from jax import lax
from jax.experimental import pallas as pl
from jax.experimental.pallas import tpu as pltpu
from jax.sharding import PartitionSpec as P

DEGREE = 4

lower_edge = 1.0
upper_edge = 6.5
HALF = (upper_edge - lower_edge) / 2
CENTER = (upper_edge + lower_edge) / 2

MESH = pl.DeviceIdType.MESH
NS = DEGREE + 1
LANES = 128
F32 = jnp.float32


def square(position, total):
    scaled = jnp.minimum(position, total - position).astype(F32) / (0.5 * total)
    return scaled * scaled


def kernel(
    sizes, shape, bands_ref, coef_ref, basis_ref, ritz_ref,
    cur, zm, zp, kin, packed, arrived, xrecv, ysend, yrecv, csend, crecv,
    sum_x, sum_yz,
    load_sem, zs_sem, zr_sem, xs_sem, xr_sem, ys_sem, yr_sem, cs_sem, cr_sem,
    ax_s, ax_r, ay_s, ay_r,
):
    nx, ny, nz = sizes
    nb, cx, cy, cz = shape
    rows = cy + 8
    wide = nb + 1
    gx, gy, gz = lax.axis_index("gx"), lax.axis_index("gy"), lax.axis_index("gz")

    def dev(dx, dy, dz):
        return (lax.rem(gx + dx + nx, nx), lax.rem(gy + dy + ny, ny), lax.rem(gz + dz + nz, nz))

    load = pltpu.make_async_copy(bands_ref, cur.at[0, 0:nb, 1 : cx + 1, 0:cy], load_sem)
    load.start()

    barrier = pltpu.get_barrier_semaphore()
    greeted = [dev(k, 0, 0) for k in range(1, nx)]
    others = [(j, k) for j in range(ny) for k in range(nz) if (j, k) != (0, 0)]
    greeted += [dev(0, j, k) for j, k in others]
    greeted += [dev(dx, dy, 0) for dx in (-1, 1) for dy in (-1, 1)]
    for target in greeted:
        pl.semaphore_signal(barrier, inc=1, device_id=target, device_id_type=MESH)

    lane = lax.broadcasted_iota(jnp.int32, (cy, LANES), 1)
    row = lax.broadcasted_iota(jnp.int32, (cy, LANES), 0)
    group = lax.rem(lane, 32)
    fy = square(row + gy * cy, ny * cy)
    kin[0] = fy + square(lane + gz * cz, nz * cz)
    strip_z = gz * cz + jnp.where(group < 16, group - 8, group + (cz - 24)) + nz * cz
    kin[1] = fy + square(lax.rem(strip_z, nz * cz), nz * cz)

    load.wait()

    half_rows = cy // 2

    def pick_strip(plane):
        result = jnp.zeros((cy, LANES), F32)
        for b in range(nb):
            v = cur[0, b, plane, 0:cy, :]
            left = pltpu.roll(v, (32 * b + 8) % LANES, 1)
            right = pltpu.roll(v, (32 * b + 24) % LANES, 1)
            mine = jnp.where(group < 16, left, right)
            result = jnp.where(lane // 32 == b, mine, result)
        return result

    outer = (group < 8) | (group >= 24)
    outer_half = outer[0:half_rows]

    @pl.loop(0, cx)
    def _(i):
        own = pick_strip(i + 1)
        cur[0, nb, i + 1, 0:cy, :] = own
        packed[i] = jnp.where(
            outer_half, own[0:half_rows], pltpu.roll(own[half_rows:cy], 16, 1)
        )

    pl.semaphore_wait(barrier, len(greeted))

    z_copy = pltpu.make_async_remote_copy(
        src_ref=packed, dst_ref=arrived, send_sem=zs_sem, recv_sem=zr_sem,
        device_id=dev(0, 0, 1), device_id_type=MESH,
    )
    z_copy.start()
    z_copy.wait()

    @pl.loop(0, cx)
    def _(i):
        there = arrived[i]
        own = cur[0, nb, i + 1, 0:cy, :]
        full = jnp.concatenate([there, pltpu.roll(there, LANES - 16, 1)], axis=0)
        cur[0, nb, i + 1, 0:cy, :] = jnp.where(outer, full, own)

    def start_sends(step):
        now = step % 2
        copies = []

        @pl.loop(0, wide)
        def _(b):
            for p in range(1, cx + 1):
                ysend[step, 0, b, p : p + 1, :] = cur[now, b, p, 0:1, :]
                ysend[step, 1, b, p : p + 1, :] = cur[now, b, p, cy - 1 : cy, :]
            for i, p in enumerate((1, cx)):
                for j, r in enumerate((0, cy - 1)):
                    csend[step, i, j, pl.ds(b, 1), :] = cur[now, b, p, r : r + 1, :]

        for i, p in enumerate((1, cx)):
            copies.append(pltpu.make_async_remote_copy(
                src_ref=cur.at[now, :, p, 0:cy], dst_ref=xrecv.at[step, i],
                send_sem=xs_sem.at[step, i], recv_sem=xr_sem.at[step, i],
                device_id=dev(2 * i - 1, 0, 0), device_id_type=MESH,
            ))
        for j in range(2):
            copies.append(pltpu.make_async_remote_copy(
                src_ref=ysend.at[step, j], dst_ref=yrecv.at[step, j],
                send_sem=ys_sem.at[step, j], recv_sem=yr_sem.at[step, j],
                device_id=dev(0, 2 * j - 1, 0), device_id_type=MESH,
            ))
        for i in range(2):
            for j in range(2):
                copies.append(pltpu.make_async_remote_copy(
                    src_ref=csend.at[step, i, j], dst_ref=crecv.at[step, i, j],
                    send_sem=cs_sem.at[step, 2 * i + j], recv_sem=cr_sem.at[step, 2 * i + j],
                    device_id=dev(2 * i - 1, 2 * j - 1, 0), device_id_type=MESH,
                ))
        for copy in copies:
            copy.start()
        return copies

    def shift_z(now, plane, first, count):
        part = pl.ds(first, count)
        at = lax.broadcasted_iota(jnp.int32, (count, LANES), 1)
        strip = cur[now, nb, plane, part, :]
        zm[nb, plane, part, :] = pltpu.roll(strip, 1, 1)
        zp[nb, plane, part, :] = pltpu.roll(strip, LANES - 1, 1)
        for b in range(nb):
            v = cur[now, b, plane, part, :]
            before = pltpu.roll(strip, (LANES - 32 * b - 7) % LANES, 1)
            after = pltpu.roll(strip, (LANES - 1 - 32 * b - 24) % LANES, 1)
            zm[b, plane, part, :] = jnp.where(at == 0, before, pltpu.roll(v, 1, 1))
            zp[b, plane, part, :] = jnp.where(at == LANES - 1, after, pltpu.roll(v, LANES - 1, 1))

    def apply_plane(step, b, plane):
        now, later = step % 2, 1 - step % 2
        fields = (zm, cur.at[now], zp)
        sums = []
        for y in range(3):
            total = None
            for x in range(3):
                for z in range(3):
                    c = coef_ref[9 * x + 3 * y + z]
                    span = pl.ds(0, cy) if y == 1 else pl.ds(0, rows)
                    term = c * fields[z][b, plane + (x - 1), span, :]
                    total = term if total is None else total + term
            sums.append(total)
        v = cur[now, b, plane, 0:cy, :]
        scale = 1.0 / HALF if step == 0 else (2.0 / HALF if step < DEGREE else 1.0)
        fx = square(gx * cx + plane - 1, nx * cx)
        if step < DEGREE:
            fx = fx - CENTER
        total = sums[1] + pltpu.roll(sums[0], 1, 0)[0:cy] + pltpu.roll(sums[2], rows - 1, 0)[0:cy]
        total = (total + (kin[b // nb] + fx) * v) * scale
        if 0 < step < DEGREE:
            total = total - cur[later, b, plane, 0:cy, :]
        cur[later, b, plane, 0:cy, :] = total

    gram_pairs = [(p, q) for p in range(nb) for q in range(p + 1)]
    pairs = [(p, q) for p in range(nb) for q in range(nb)]
    fslot, hslot = DEGREE % 2, 1 - DEGREE % 2

    def fold(a):
        total = a[0:8]
        for k in range(8, cy, 8):
            total = total + a[k : k + 8]
        return total

    copies = start_sends(0)
    for step in range(NS):
        now = step % 2
        live = wide if step < DEGREE else nb
        x_copies, y_copies, c_copies = copies[0:2], copies[2:4], copies[4:8]

        @pl.loop(1, cx + 1)
        def _(p):
            shift_z(now, p, 0, cy)

        if step == DEGREE:
            def gram_plane(p, acc):
                f = [cur[fslot, b, p + 1, 0:cy, :] for b in range(nb)]
                return tuple(a + fold(f[i] * f[j]) for a, (i, j) in zip(acc, gram_pairs))

            grams = lax.fori_loop(
                0, cx, gram_plane, tuple(jnp.zeros((8, LANES), F32) for _ in gram_pairs)
            )

        for copy in y_copies:
            copy.wait_recv()

        @pl.loop(0, wide)
        def _(b):
            for p in range(1, cx + 1):
                cur[now, b, p, cy : cy + 1, :] = yrecv[step, 0, b, p : p + 1, :]
                cur[now, b, p, rows - 1 : rows, :] = yrecv[step, 1, b, p : p + 1, :]

        @pl.loop(1, cx + 1)
        def _(p):
            shift_z(now, p, cy, 8)

        @pl.loop(0, live * (cx - 2))
        def _(t):
            apply_plane(step, t // (cx - 2), lax.rem(t, cx - 2) + 2)

        for copy in x_copies + c_copies:
            copy.wait_recv()

        @pl.loop(0, wide)
        def _(b):
            for i, p in enumerate((cx + 1, 0)):
                cur[now, b, p, 0:cy, :] = xrecv[step, i, b]
                cur[now, b, p, cy : cy + 1, :] = crecv[step, i, 0, pl.ds(b, 1), :]
                cur[now, b, p, rows - 1 : rows, :] = crecv[step, i, 1, pl.ds(b, 1), :]

        for p in (0, cx + 1):
            shift_z(now, p, 0, rows)

        @pl.loop(0, live)
        def _(b):
            apply_plane(step, b, 1)
            apply_plane(step, b, cx)

        for copy in copies:
            copy.wait_send()
        if step < DEGREE:
            copies = start_sends(step + 1)

    def dot_plane(p, acc):
        f = [cur[fslot, b, p + 1, 0:cy, :] for b in range(nb)]
        h = [cur[hslot, b, p + 1, 0:cy, :] for b in range(nb)]
        return tuple(a + fold(f[i] * h[j]) for a, (i, j) in zip(acc, pairs))

    dots = lax.fori_loop(0, cx, dot_plane, tuple(jnp.zeros((8, LANES), F32) for _ in pairs))
    everything = list(grams) + list(dots)
    slot = lax.broadcasted_iota(jnp.int32, (8, LANES), 0)
    quarter = lax.broadcasted_iota(jnp.int32, (8, LANES), 1) // 32
    payload = jnp.zeros((8, LANES), F32)
    for start in range(0, len(everything), 8):
        tile = jnp.zeros((8, LANES), F32)
        for k, part in enumerate(everything[start : start + 8]):
            tile = jnp.where(slot == k, jnp.sum(part, axis=0, keepdims=True), tile)
        tile = tile + pltpu.roll(tile, 64, 1)
        tile = tile + pltpu.roll(tile, 32, 1)
        payload = jnp.where(quarter == start // 8, tile, payload)

    def reduce_over(value, buffer, place, targets, send_sem, recv_sem):
        buffer[place] = value
        sends = []
        for k, target in enumerate(targets):
            sends.append(pltpu.make_async_remote_copy(
                src_ref=buffer.at[place], dst_ref=buffer.at[place],
                send_sem=send_sem.at[k], recv_sem=recv_sem.at[k],
                device_id=target, device_id_type=MESH,
            ))
        for copy in sends:
            copy.start()
        for copy in sends:
            copy.wait()
        total = buffer[0]
        for k in range(1, len(targets) + 1):
            total = total + buffer[k]
        return total

    value = reduce_over(payload, sum_x, gx, greeted[: nx - 1], ax_s, ax_r)
    value = reduce_over(
        value, sum_yz, gy * nz + gz, greeted[nx - 1 : nx - 1 + len(others)], ay_s, ay_r
    )
    value = value * (1.0 / (nx * ny * nz * cx * cy * cz))
    columns = [
        jnp.broadcast_to(
            jnp.sum(jnp.where(quarter == j, value, 0.0), axis=1, keepdims=True), (8, LANES)
        )
        for j in range((len(everything) + 7) // 8)
    ]

    def entry(k):
        return columns[k // 8][k % 8 : k % 8 + 1]

    gram = {pair: entry(k) for k, pair in enumerate(gram_pairs)}
    product = {pair: entry(k + len(gram_pairs)) for k, pair in enumerate(pairs)}
    low, recip = {}, []
    for q in range(nb):
        s = gram[q, q]
        for k in range(q):
            s = s - low[q, k] * low[q, k]
        recip.append(1.0 / jnp.sqrt(s))
        for p in range(q + 1, nb):
            s = gram[p, q]
            for k in range(q):
                s = s - low[p, k] * low[q, k]
            low[p, q] = s * recip[q]
    inv = {}
    for q in range(nb):
        inv[q, q] = recip[q]
        for p in range(q + 1, nb):
            s = low[p, q] * inv[q, q]
            for k in range(q + 1, p):
                s = s + low[p, k] * inv[k, q]
            inv[p, q] = -s * recip[p]

    @pl.loop(0, cx)
    def _(i):
        f = [cur[fslot, b, i + 1, 0:cy, :] for b in range(nb)]
        for p in range(nb):
            total = inv[p, 0] * f[0]
            for q in range(1, p + 1):
                total = total + inv[p, q] * f[q]
            basis_ref[p, i] = total

    left = {}
    for p in range(nb):
        for s in range(nb):
            total = inv[p, 0] * product[0, s]
            for r in range(1, p + 1):
                total = total + inv[p, r] * product[r, s]
            left[p, s] = total
    at_row = lax.broadcasted_iota(jnp.int32, (8, LANES), 0)
    at_lane = lax.broadcasted_iota(jnp.int32, (8, LANES), 1)
    ritz = jnp.zeros((8, LANES), F32)
    for p in range(nb):
        for q in range(nb):
            total = left[p, 0] * inv[q, 0]
            for s in range(1, q + 1):
                total = total + left[p, s] * inv[q, s]
            ritz = jnp.where((at_row == p) & (at_lane == q), total, ritz)
    ritz_ref[...] = ritz[0:nb, 0:nb]


def local(sizes, bands, stencil_coef):
    nx, ny, nz = sizes
    nb, cx, cy, cz = shape = bands.shape
    assert nz == 2 and cz == LANES and cy % 16 == 0 and nb == 4 and nx > 2
    wide, rows, nyz = nb + 1, cy + 8, ny * nz
    up = -(-(cx + 2) // 8) * 8
    dma = pltpu.SemaphoreType.DMA
    return pl.pallas_call(
        functools.partial(kernel, sizes, shape),
        out_shape=(
            jax.ShapeDtypeStruct(shape, F32),
            jax.ShapeDtypeStruct((nb, nb), F32),
        ),
        in_specs=[
            pl.BlockSpec(memory_space=pl.ANY),
            pl.BlockSpec(memory_space=pltpu.SMEM),
        ],
        out_specs=(
            pl.BlockSpec(memory_space=pltpu.VMEM),
            pl.BlockSpec(memory_space=pltpu.VMEM),
        ),
        scratch_shapes=[
            pltpu.VMEM((2, wide, cx + 2, rows, LANES), F32),
            pltpu.VMEM((wide, cx + 2, rows, LANES), F32),
            pltpu.VMEM((wide, cx + 2, rows, LANES), F32),
            pltpu.VMEM((2, cy, LANES), F32),
            pltpu.VMEM((cx, cy // 2, LANES), F32),
            pltpu.VMEM((cx, cy // 2, LANES), F32),
            pltpu.VMEM((NS, 2, wide, cy, LANES), F32),
            pltpu.VMEM((NS, 2, wide, up, LANES), F32),
            pltpu.VMEM((NS, 2, wide, up, LANES), F32),
            pltpu.VMEM((NS, 2, 2, 8, LANES), F32),
            pltpu.VMEM((NS, 2, 2, 8, LANES), F32),
            pltpu.VMEM((nx, 8, LANES), F32),
            pltpu.VMEM((nyz, 8, LANES), F32),
            dma, dma, dma,
            dma((NS, 2)), dma((NS, 2)),
            dma((NS, 2)), dma((NS, 2)),
            dma((NS, 4)), dma((NS, 4)),
            dma((nx - 1,)), dma((nx - 1,)),
            dma((nyz - 1,)), dma((nyz - 1,)),
        ],
        compiler_params=pltpu.CompilerParams(
            collective_id=0, has_side_effects=True, vmem_limit_bytes=40 * 1024 * 1024
        ),
    )(bands, stencil_coef)


def solution(mesh):
    placed = (P(None, "gx", "gy", "gz"), P())
    sizes = (mesh.shape["gx"], mesh.shape["gy"], mesh.shape["gz"])
    return jax.shard_map(
        functools.partial(local, sizes),
        mesh=mesh,
        in_specs=placed,
        out_specs=placed,
        check_vma=False,
    )
```

```python
import functools

import jax
import jax.numpy as jnp
from jax import lax
from jax.experimental import pallas as pl
from jax.experimental.pallas import tpu as pltpu
from jax.sharding import PartitionSpec as P

DEGREE = 4

lower_edge = 1.0
upper_edge = 6.5
HALF = (upper_edge - lower_edge) / 2
CENTER = (upper_edge + lower_edge) / 2

MESH = pl.DeviceIdType.MESH
NS = DEGREE + 1
LANES = 128
F32 = jnp.float32


def square(position, total):
    scaled = jnp.minimum(position, total - position).astype(F32) / (0.5 * total)
    return scaled * scaled


def kernel(
    sizes, shape, bands_ref, coef_ref, basis_ref, ritz_ref,
    cur, zm, zp, kin, packed, arrived, xrecv, ysend, yrecv, csend, crecv,
    sum_x, sum_yz, pick,
    load_sem, zs_sem, zr_sem, xs_sem, xr_sem, ys_sem, yr_sem, cs_sem, cr_sem,
    ax_s, ax_r, ay_s, ay_r,
):
    nx, ny, nz = sizes
    nb, cx, cy, cz = shape
    rows = cy + 8
    wide = nb + 1
    gx, gy, gz = lax.axis_index("gx"), lax.axis_index("gy"), lax.axis_index("gz")

    def dev(dx, dy, dz):
        return (lax.rem(gx + dx + nx, nx), lax.rem(gy + dy + ny, ny), lax.rem(gz + dz + nz, nz))

    load = pltpu.make_async_copy(bands_ref, cur.at[0, 0:nb, 1 : cx + 1, 0:cy], load_sem)
    load.start()

    barrier = pltpu.get_barrier_semaphore()
    greeted = [dev(k, 0, 0) for k in range(1, nx)]
    others = [(j, k) for j in range(ny) for k in range(nz) if (j, k) != (0, 0)]
    greeted += [dev(0, j, k) for j, k in others]
    greeted += [dev(dx, dy, 0) for dx in (-1, 1) for dy in (-1, 1)]
    for target in greeted:
        pl.semaphore_signal(barrier, inc=1, device_id=target, device_id_type=MESH)

    lane = lax.broadcasted_iota(jnp.int32, (cy, LANES), 1)
    row = lax.broadcasted_iota(jnp.int32, (cy, LANES), 0)
    group = lax.rem(lane, 32)
    fy = square(row + gy * cy, ny * cy)
    kin[0] = fy + square(lane + gz * cz, nz * cz)
    strip_z = gz * cz + jnp.where(group < 16, group - 8, group + (cz - 24)) + nz * cz
    kin[1] = fy + square(lax.rem(strip_z, nz * cz), nz * cz)

    take = lax.broadcasted_iota(jnp.int32, (2 * LANES, 2 * LANES), 0)
    give = lax.broadcasted_iota(jnp.int32, (2 * LANES, 2 * LANES), 1)
    inside = ((give < LANES) & (take == give - 1)) | (
        (give >= LANES) & (take < LANES) & (take == give - LANES + 1)
    )
    for b in range(nb):
        before = (give == 0) & (take == LANES + 32 * b + 7)
        after = (give == 2 * LANES - 1) & (take == LANES + 32 * b + 24)
        pick[b] = jnp.where(inside | before | after, 1.0, 0.0).astype(jnp.bfloat16)

    load.wait()

    half_rows = cy // 2

    def pick_strip(plane):
        result = jnp.zeros((cy, LANES), F32)
        for b in range(nb):
            v = cur[0, b, plane, 0:cy, :]
            left = pltpu.roll(v, (32 * b + 8) % LANES, 1)
            right = pltpu.roll(v, (32 * b + 24) % LANES, 1)
            mine = jnp.where(group < 16, left, right)
            result = jnp.where(lane // 32 == b, mine, result)
        return result

    outer = (group < 8) | (group >= 24)
    outer_half = outer[0:half_rows]

    @pl.loop(0, cx)
    def _(i):
        own = pick_strip(i + 1)
        cur[0, nb, i + 1, 0:cy, :] = own
        packed[i] = jnp.where(
            outer_half, own[0:half_rows], pltpu.roll(own[half_rows:cy], 16, 1)
        )

    pl.semaphore_wait(barrier, len(greeted))

    def parts(step):
        return ((nb, wide), (0, nb)) if step == 0 else ((2, wide), (0, 2))

    def x_sends(step, g):
        now = step % 2
        first, last = parts(step)[g]
        copies = []
        for i, p in enumerate((1, cx)):
            copies.append(pltpu.make_async_remote_copy(
                src_ref=cur.at[now, first:last, p, 0:cy], dst_ref=xrecv.at[step, i, first:last],
                send_sem=xs_sem.at[step, g, i], recv_sem=xr_sem.at[step, g, i],
                device_id=dev(2 * i - 1, 0, 0), device_id_type=MESH,
            ))
            copies[-1].start()
        for i, p in enumerate((1, cx)):
            for j, r in enumerate((0, cy - 1)):
                for b in range(first, last):
                    csend[step, g, i, j, b : b + 1, :] = cur[now, b, p, r : r + 1, :]
                copies.append(pltpu.make_async_remote_copy(
                    src_ref=csend.at[step, g, i, j], dst_ref=crecv.at[step, g, i, j],
                    send_sem=cs_sem.at[step, g, 2 * i + j], recv_sem=cr_sem.at[step, g, 2 * i + j],
                    device_id=dev(2 * i - 1, 2 * j - 1, 0), device_id_type=MESH,
                ))
                copies[-1].start()
        return copies

    def y_sends(step):
        now = step % 2
        copies = []

        @pl.loop(0, wide)
        def _(b):
            for p in range(1, cx + 1):
                ysend[step, 0, b, p : p + 1, :] = cur[now, b, p, 0:1, :]
                ysend[step, 1, b, p : p + 1, :] = cur[now, b, p, cy - 1 : cy, :]

        for j in range(2):
            copies.append(pltpu.make_async_remote_copy(
                src_ref=ysend.at[step, j], dst_ref=yrecv.at[step, j],
                send_sem=ys_sem.at[step, j], recv_sem=yr_sem.at[step, j],
                device_id=dev(0, 2 * j - 1, 0), device_id_type=MESH,
            ))
            copies[-1].start()
        return copies

    z_copy = pltpu.make_async_remote_copy(
        src_ref=packed, dst_ref=arrived, send_sem=zs_sem, recv_sem=zr_sem,
        device_id=dev(0, 0, 1), device_id_type=MESH,
    )
    z_copy.start()
    x_copies = [None, x_sends(0, 1)]
    z_copy.wait()

    @pl.loop(0, cx)
    def _(i):
        there = arrived[i]
        own = cur[0, nb, i + 1, 0:cy, :]
        full = jnp.concatenate([there, pltpu.roll(there, LANES - 16, 1)], axis=0)
        cur[0, nb, i + 1, 0:cy, :] = jnp.where(outer, full, own)

    def halves(v):
        high = v.astype(jnp.bfloat16)
        low = (v - high.astype(F32)).astype(jnp.bfloat16)
        return jnp.concatenate([high, low], axis=0)

    def shift_z(now, plane, planes, first, count, band=0, end=None):
        part, which = pl.ds(first, count), pl.ds(plane, planes)
        m = planes * count
        strip = cur[now, nb, which, part, :].reshape(m, LANES)
        end = wide if end is None else end
        if end == wide:
            zm[nb, which, part, :] = pltpu.roll(strip, 1, 1).reshape(planes, count, LANES)
            zp[nb, which, part, :] = pltpu.roll(strip, LANES - 1, 1).reshape(planes, count, LANES)
        strip = halves(strip)
        for b in range(band, min(end, nb)):
            v = halves(cur[now, b, which, part, :].reshape(m, LANES))
            moved = jnp.dot(
                jnp.concatenate([v, strip], axis=1), pick[b], preferred_element_type=F32
            )
            moved = moved[0:m] + moved[m : 2 * m]
            zm[b, which, part, :] = moved[:, 0:LANES].reshape(planes, count, LANES)
            zp[b, which, part, :] = moved[:, LANES:].reshape(planes, count, LANES)

    def apply_plane(step, b, plane):
        now, later = step % 2, 1 - step % 2
        fields = (zm, cur.at[now], zp)
        sums = []
        for y in range(3):
            total = None
            for x in range(3):
                for z in range(3):
                    c = coef_ref[9 * x + 3 * y + z]
                    span = pl.ds(0, cy) if y == 1 else pl.ds(0, rows)
                    term = c * fields[z][b, plane + (x - 1), span, :]
                    total = term if total is None else total + term
            sums.append(total)
        v = cur[now, b, plane, 0:cy, :]
        scale = 1.0 / HALF if step == 0 else (2.0 / HALF if step < DEGREE else 1.0)
        fx = square(gx * cx + plane - 1, nx * cx)
        if step < DEGREE:
            fx = fx - CENTER
        total = sums[1] + pltpu.roll(sums[0], 1, 0)[0:cy] + pltpu.roll(sums[2], rows - 1, 0)[0:cy]
        total = (total + (kin[b // nb] + fx) * v) * scale
        if 0 < step < DEGREE:
            total = total - cur[later, b, plane, 0:cy, :]
        cur[later, b, plane, 0:cy, :] = total

    gram_pairs = [(p, q) for p in range(nb) for q in range(p + 1)]
    pairs = [(p, q) for p in range(nb) for q in range(nb)]
    fslot, hslot = DEGREE % 2, 1 - DEGREE % 2

    def fold(a):
        total = a[0:8]
        for k in range(8, cy, 8):
            total = total + a[k : k + 8]
        return total

    x_copies[0] = x_sends(0, 0)
    y_copies = y_sends(0)
    for step in range(NS):
        now = step % 2
        live = wide if step < DEGREE else nb

        @pl.loop(0, cx // 4)
        def _(i):
            shift_z(now, 4 * i + 1, 4, 0, cy)

        if step == DEGREE:
            def gram_plane(p, acc):
                f = [cur[fslot, b, p + 1, 0:cy, :] for b in range(nb)]
                return tuple(a + fold(f[i] * f[j]) for a, (i, j) in zip(acc, gram_pairs))

            grams = lax.fori_loop(
                0, cx, gram_plane, tuple(jnp.zeros((8, LANES), F32) for _ in gram_pairs)
            )

        for copy in y_copies:
            copy.wait_recv()

        @pl.loop(0, wide)
        def _(b):
            for p in range(1, cx + 1):
                cur[now, b, p, cy : cy + 1, :] = yrecv[step, 0, b, p : p + 1, :]
                cur[now, b, p, rows - 1 : rows, :] = yrecv[step, 1, b, p : p + 1, :]

        shift_z(now, 1, cx, cy, 8)

        @pl.loop(0, live * (cx - 2))
        def _(t):
            apply_plane(step, t // (cx - 2), lax.rem(t, cx - 2) + 2)

        later_x = []
        for copy in y_copies + x_copies[0][:2] + x_copies[1][:2]:
            copy.wait_send()
        for g, (first, last) in enumerate(parts(max(step, 1))):
            need = x_copies if step == 0 and g == 0 else ([] if step == 0 else [x_copies[g]])
            for copy in sum(need, []):
                copy.wait_recv()
            for b in range(first, last):
                source = g if step > 0 else (0 if b == nb else 1)
                for i, p in enumerate((cx + 1, 0)):
                    cur[now, b, p, 0:cy, :] = xrecv[step, i, b]
                    cur[now, b, p, cy : cy + 1, :] = crecv[step, source, i, 0, b : b + 1, :]
                    cur[now, b, p, rows - 1 : rows, :] = crecv[step, source, i, 1, b : b + 1, :]
            for p in (0, cx + 1):
                shift_z(now, p, 1, 0, rows, first, last)

            @pl.loop(first, min(last, live))
            def _(b):
                apply_plane(step, b, 1)
                apply_plane(step, b, cx)

            if step < DEGREE:
                later_x.append(x_sends(step + 1, g))
        for copy in x_copies[0][2:] + x_copies[1][2:]:
            copy.wait_send()
        x_copies = later_x
        if step < DEGREE:
            y_copies = y_sends(step + 1)

    def dot_plane(p, acc):
        f = [cur[fslot, b, p + 1, 0:cy, :] for b in range(nb)]
        h = [cur[hslot, b, p + 1, 0:cy, :] for b in range(nb)]
        return tuple(a + fold(f[i] * h[j]) for a, (i, j) in zip(acc, pairs))

    dots = lax.fori_loop(0, cx, dot_plane, tuple(jnp.zeros((8, LANES), F32) for _ in pairs))
    everything = list(grams) + list(dots)
    slot = lax.broadcasted_iota(jnp.int32, (8, LANES), 0)
    quarter = lax.broadcasted_iota(jnp.int32, (8, LANES), 1) // 32
    payload = jnp.zeros((8, LANES), F32)
    for start in range(0, len(everything), 8):
        tile = jnp.zeros((8, LANES), F32)
        for k, part in enumerate(everything[start : start + 8]):
            tile = jnp.where(slot == k, jnp.sum(part, axis=0, keepdims=True), tile)
        tile = tile + pltpu.roll(tile, 64, 1)
        tile = tile + pltpu.roll(tile, 32, 1)
        payload = jnp.where(quarter == start // 8, tile, payload)

    def reduce_over(value, buffer, place, targets, send_sem, recv_sem):
        buffer[place] = value
        sends = []
        for k, target in enumerate(targets):
            sends.append(pltpu.make_async_remote_copy(
                src_ref=buffer.at[place], dst_ref=buffer.at[place],
                send_sem=send_sem.at[k], recv_sem=recv_sem.at[k],
                device_id=target, device_id_type=MESH,
            ))
        for copy in sends:
            copy.start()
        for copy in sends:
            copy.wait()
        total = buffer[0]
        for k in range(1, len(targets) + 1):
            total = total + buffer[k]
        return total

    value = reduce_over(payload, sum_x, gx, greeted[: nx - 1], ax_s, ax_r)
    value = reduce_over(
        value, sum_yz, gy * nz + gz, greeted[nx - 1 : nx - 1 + len(others)], ay_s, ay_r
    )
    value = value * (1.0 / (nx * ny * nz * cx * cy * cz))
    columns = [
        jnp.broadcast_to(
            jnp.sum(jnp.where(quarter == j, value, 0.0), axis=1, keepdims=True), (8, LANES)
        )
        for j in range((len(everything) + 7) // 8)
    ]

    def entry(k):
        return columns[k // 8][k % 8 : k % 8 + 1]

    gram = {pair: entry(k) for k, pair in enumerate(gram_pairs)}
    product = {pair: entry(k + len(gram_pairs)) for k, pair in enumerate(pairs)}
    low, recip = {}, []
    for q in range(nb):
        s = gram[q, q]
        for k in range(q):
            s = s - low[q, k] * low[q, k]
        recip.append(1.0 / jnp.sqrt(s))
        for p in range(q + 1, nb):
            s = gram[p, q]
            for k in range(q):
                s = s - low[p, k] * low[q, k]
            low[p, q] = s * recip[q]
    inv = {}
    for q in range(nb):
        inv[q, q] = recip[q]
        for p in range(q + 1, nb):
            s = low[p, q] * inv[q, q]
            for k in range(q + 1, p):
                s = s + low[p, k] * inv[k, q]
            inv[p, q] = -s * recip[p]

    @pl.loop(0, cx)
    def _(i):
        f = [cur[fslot, b, i + 1, 0:cy, :] for b in range(nb)]
        for p in range(nb):
            total = inv[p, 0] * f[0]
            for q in range(1, p + 1):
                total = total + inv[p, q] * f[q]
            basis_ref[p, i] = total

    left = {}
    for p in range(nb):
        for s in range(nb):
            total = inv[p, 0] * product[0, s]
            for r in range(1, p + 1):
                total = total + inv[p, r] * product[r, s]
            left[p, s] = total
    at_row = lax.broadcasted_iota(jnp.int32, (8, LANES), 0)
    at_lane = lax.broadcasted_iota(jnp.int32, (8, LANES), 1)
    ritz = jnp.zeros((8, LANES), F32)
    for p in range(nb):
        for q in range(nb):
            total = left[p, 0] * inv[q, 0]
            for s in range(1, q + 1):
                total = total + left[p, s] * inv[q, s]
            ritz = jnp.where((at_row == p) & (at_lane == q), total, ritz)
    ritz_ref[...] = ritz[0:nb, 0:nb]


def local(sizes, bands, stencil_coef):
    nx, ny, nz = sizes
    nb, cx, cy, cz = shape = bands.shape
    assert nz == 2 and cz == LANES and cy % 16 == 0 and nb == 4 and nx > 2 and cx % 4 == 0
    wide, rows, nyz = nb + 1, cy + 8, ny * nz
    up = -(-(cx + 2) // 8) * 8
    dma = pltpu.SemaphoreType.DMA
    return pl.pallas_call(
        functools.partial(kernel, sizes, shape),
        out_shape=(
            jax.ShapeDtypeStruct(shape, F32),
            jax.ShapeDtypeStruct((nb, nb), F32),
        ),
        in_specs=[
            pl.BlockSpec(memory_space=pl.ANY),
            pl.BlockSpec(memory_space=pltpu.SMEM),
        ],
        out_specs=(
            pl.BlockSpec(memory_space=pltpu.VMEM),
            pl.BlockSpec(memory_space=pltpu.VMEM),
        ),
        scratch_shapes=[
            pltpu.VMEM((2, wide, cx + 2, rows, LANES), F32),
            pltpu.VMEM((wide, cx + 2, rows, LANES), F32),
            pltpu.VMEM((wide, cx + 2, rows, LANES), F32),
            pltpu.VMEM((2, cy, LANES), F32),
            pltpu.VMEM((cx, cy // 2, LANES), F32),
            pltpu.VMEM((cx, cy // 2, LANES), F32),
            pltpu.VMEM((NS, 2, wide, cy, LANES), F32),
            pltpu.VMEM((NS, 2, wide, up, LANES), F32),
            pltpu.VMEM((NS, 2, wide, up, LANES), F32),
            pltpu.VMEM((NS, 2, 2, 2, 8, LANES), F32),
            pltpu.VMEM((NS, 2, 2, 2, 8, LANES), F32),
            pltpu.VMEM((nx, 8, LANES), F32),
            pltpu.VMEM((nyz, 8, LANES), F32),
            pltpu.VMEM((nb, 2 * LANES, 2 * LANES), jnp.bfloat16),
            dma, dma, dma,
            dma((NS, 2, 2)), dma((NS, 2, 2)),
            dma((NS, 2)), dma((NS, 2)),
            dma((NS, 2, 4)), dma((NS, 2, 4)),
            dma((nx - 1,)), dma((nx - 1,)),
            dma((nyz - 1,)), dma((nyz - 1,)),
        ],
        compiler_params=pltpu.CompilerParams(
            collective_id=0, has_side_effects=True, vmem_limit_bytes=40 * 1024 * 1024
        ),
    )(bands, stencil_coef)


def solution(mesh):
    placed = (P(None, "gx", "gy", "gz"), P())
    sizes = (mesh.shape["gx"], mesh.shape["gy"], mesh.shape["gz"])
    return jax.shard_map(
        functools.partial(local, sizes),
        mesh=mesh,
        in_specs=placed,
        out_specs=placed,
        check_vma=False,
    )
```

```python
import functools

import jax
import jax.numpy as jnp
from jax import lax
from jax.experimental import pallas as pl
from jax.experimental.pallas import tpu as pltpu
from jax.sharding import PartitionSpec as P

DEGREE = 4

lower_edge = 1.0
upper_edge = 6.5
HALF = (upper_edge - lower_edge) / 2
CENTER = (upper_edge + lower_edge) / 2

MESH = pl.DeviceIdType.MESH
NS = DEGREE + 1
LANES = 128
F32 = jnp.float32


def square(position, total):
    scaled = jnp.minimum(position, total - position).astype(F32) / (0.5 * total)
    return scaled * scaled


def kernel(
    sizes, shape, bands_ref, coef_ref, basis_ref, ritz_ref,
    cur, zm, zp, kin, packed, arrived, xrecv, ysend, yrecv, csend, crecv,
    sum_x, sum_yz, pick, edge_coef,
    load_sem, zs_sem, zr_sem, xs_sem, xr_sem, ys_sem, yr_sem, cs_sem, cr_sem,
    ax_s, ax_r, ay_s, ay_r,
):
    nx, ny, nz = sizes
    nb, cx, cy, cz = shape
    rows = cy + 8
    wide = nb + 1
    gx, gy, gz = lax.axis_index("gx"), lax.axis_index("gy"), lax.axis_index("gz")

    def dev(dx, dy, dz):
        return (lax.rem(gx + dx + nx, nx), lax.rem(gy + dy + ny, ny), lax.rem(gz + dz + nz, nz))

    load = pltpu.make_async_copy(bands_ref, cur.at[0, 0:nb, 1 : cx + 1, 0:cy], load_sem)
    load.start()

    barrier = pltpu.get_barrier_semaphore()
    greeted = [dev(k, 0, 0) for k in range(1, nx)]
    others = [(j, k) for j in range(ny) for k in range(nz) if (j, k) != (0, 0)]
    greeted += [dev(0, j, k) for j, k in others]
    greeted += [dev(dx, dy, 0) for dx in (-1, 1) for dy in (-1, 1)]
    for target in greeted:
        pl.semaphore_signal(barrier, inc=1, device_id=target, device_id_type=MESH)

    lane = lax.broadcasted_iota(jnp.int32, (cy, LANES), 1)
    row = lax.broadcasted_iota(jnp.int32, (cy, LANES), 0)
    group = lax.rem(lane, 32)
    fy = square(row + gy * cy, ny * cy)
    kin[0] = fy + square(lane + gz * cz, nz * cz)
    strip_z = gz * cz + jnp.where(group < 16, group - 8, group + (cz - 24)) + nz * cz
    kin[1] = fy + square(lax.rem(strip_z, nz * cz), nz * cz)

    take = lax.broadcasted_iota(jnp.int32, (2 * LANES, 2 * LANES), 0)
    give = lax.broadcasted_iota(jnp.int32, (2 * LANES, 2 * LANES), 1)
    inside = ((give < LANES) & (take == give - 1)) | (
        (give >= LANES) & (take < LANES) & (take == give - LANES + 1)
    )
    for b in range(nb):
        before = (give == 0) & (take == LANES + 32 * b + 7)
        after = (give == 2 * LANES - 1) & (take == LANES + 32 * b + 24)
        pick[b] = jnp.where(inside | before | after, 1.0, 0.0).astype(jnp.bfloat16)

    tile_row = lax.broadcasted_iota(jnp.int32, (8, LANES), 0)
    for x in range(3):
        for z in range(3):
            edge_coef[3 * x + z] = jnp.where(
                tile_row < 4, coef_ref[9 * x + 6 + z], coef_ref[9 * x + z]
            )

    load.wait()

    half_rows = cy // 2

    def pick_strip(plane):
        result = jnp.zeros((cy, LANES), F32)
        for b in range(nb):
            v = cur[0, b, plane, 0:cy, :]
            left = pltpu.roll(v, (32 * b + 8) % LANES, 1)
            right = pltpu.roll(v, (32 * b + 24) % LANES, 1)
            mine = jnp.where(group < 16, left, right)
            result = jnp.where(lane // 32 == b, mine, result)
        return result

    outer = (group < 8) | (group >= 24)
    outer_half = outer[0:half_rows]

    @pl.loop(0, cx)
    def _(i):
        own = pick_strip(i + 1)
        cur[0, nb, i + 1, 0:cy, :] = own
        packed[i] = jnp.where(
            outer_half, own[0:half_rows], pltpu.roll(own[half_rows:cy], 16, 1)
        )

    pl.semaphore_wait(barrier, len(greeted))

    def parts(step):
        return ((nb, wide), (0, nb)) if step == 0 else ((2, wide), (0, 2))

    def x_sends(step, g):
        now = step % 2
        first, last = parts(step)[g]
        copies = []
        for i, p in enumerate((1, cx)):
            copies.append(pltpu.make_async_remote_copy(
                src_ref=cur.at[now, first:last, p, 0:cy], dst_ref=xrecv.at[step, i, first:last],
                send_sem=xs_sem.at[step, g, i], recv_sem=xr_sem.at[step, g, i],
                device_id=dev(2 * i - 1, 0, 0), device_id_type=MESH,
            ))
            copies[-1].start()
        for i, p in enumerate((1, cx)):
            for j, r in enumerate((0, cy - 1)):
                for b in range(first, last):
                    csend[step, g, i, j, b : b + 1, :] = cur[now, b, p, r : r + 1, :]
                copies.append(pltpu.make_async_remote_copy(
                    src_ref=csend.at[step, g, i, j], dst_ref=crecv.at[step, g, i, j],
                    send_sem=cs_sem.at[step, g, 2 * i + j], recv_sem=cr_sem.at[step, g, 2 * i + j],
                    device_id=dev(2 * i - 1, 2 * j - 1, 0), device_id_type=MESH,
                ))
                copies[-1].start()
        return copies

    def y_sends(step, g):
        now = step % 2
        first, last = parts(step)[g]
        copies = []

        @pl.loop(first, last)
        def _(b):
            for p in range(1, cx + 1):
                ysend[step, 0, b, p : p + 1, :] = cur[now, b, p, 0:1, :]
                ysend[step, 1, b, p : p + 1, :] = cur[now, b, p, cy - 1 : cy, :]

        for j in range(2):
            copies.append(pltpu.make_async_remote_copy(
                src_ref=ysend.at[step, j, first:last], dst_ref=yrecv.at[step, j, first:last],
                send_sem=ys_sem.at[step, g, j], recv_sem=yr_sem.at[step, g, j],
                device_id=dev(0, 2 * j - 1, 0), device_id_type=MESH,
            ))
            copies[-1].start()
        return copies

    z_copy = pltpu.make_async_remote_copy(
        src_ref=packed, dst_ref=arrived, send_sem=zs_sem, recv_sem=zr_sem,
        device_id=dev(0, 0, 1), device_id_type=MESH,
    )
    z_copy.start()
    x_copies = [None, x_sends(0, 1)]
    y_copies = [None, y_sends(0, 1)]
    z_copy.wait()

    @pl.loop(0, cx)
    def _(i):
        there = arrived[i]
        own = cur[0, nb, i + 1, 0:cy, :]
        full = jnp.concatenate([there, pltpu.roll(there, LANES - 16, 1)], axis=0)
        cur[0, nb, i + 1, 0:cy, :] = jnp.where(outer, full, own)

    def halves(v):
        high = v.astype(jnp.bfloat16)
        low = (v - high.astype(F32)).astype(jnp.bfloat16)
        return jnp.concatenate([high, low], axis=0)

    def shift_z(now, plane, planes, first, count, band=0, end=None):
        part, which = pl.ds(first, count), pl.ds(plane, planes)
        m = planes * count
        strip = cur[now, nb, which, part, :].reshape(m, LANES)
        end = wide if end is None else end
        if end == wide:
            zm[nb, which, part, :] = pltpu.roll(strip, 1, 1).reshape(planes, count, LANES)
            zp[nb, which, part, :] = pltpu.roll(strip, LANES - 1, 1).reshape(planes, count, LANES)
        strip = halves(strip)
        for b in range(band, min(end, nb)):
            v = halves(cur[now, b, which, part, :].reshape(m, LANES))
            moved = jnp.dot(
                jnp.concatenate([v, strip], axis=1), pick[b], preferred_element_type=F32
            )
            moved = moved[0:m] + moved[m : 2 * m]
            zm[b, which, part, :] = moved[:, 0:LANES].reshape(planes, count, LANES)
            zp[b, which, part, :] = moved[:, LANES:].reshape(planes, count, LANES)

    def apply_plane(step, b, plane):
        now, later = step % 2, 1 - step % 2
        fields = (zm, cur.at[now], zp)
        sums = []
        for y in range(3):
            total = None
            for x in range(3):
                for z in range(3):
                    c = coef_ref[9 * x + 3 * y + z]
                    term = c * fields[z][b, plane + (x - 1), 0:cy, :]
                    total = term if total is None else total + term
            sums.append(total)
        edge = None
        for x in range(3):
            for z in range(3):
                term = edge_coef[3 * x + z] * fields[z][b, plane + (x - 1), cy:rows, :]
                edge = term if edge is None else edge + term
        sums[0] = jnp.concatenate([sums[0], edge], axis=0)
        sums[2] = jnp.concatenate([sums[2], edge], axis=0)
        v = cur[now, b, plane, 0:cy, :]
        scale = 1.0 / HALF if step == 0 else (2.0 / HALF if step < DEGREE else 1.0)
        fx = square(gx * cx + plane - 1, nx * cx)
        if step < DEGREE:
            fx = fx - CENTER
        total = sums[1] + pltpu.roll(sums[0], 1, 0)[0:cy] + pltpu.roll(sums[2], rows - 1, 0)[0:cy]
        total = (total + (kin[b // nb] + fx) * v) * scale
        if 0 < step < DEGREE:
            total = total - cur[later, b, plane, 0:cy, :]
        cur[later, b, plane, 0:cy, :] = total

    gram_pairs = [(p, q) for p in range(nb) for q in range(p + 1)]
    pairs = [(p, q) for p in range(nb) for q in range(nb)]
    fslot, hslot = DEGREE % 2, 1 - DEGREE % 2

    def fold(a):
        total = a[0:8]
        for k in range(8, cy, 8):
            total = total + a[k : k + 8]
        return total

    x_copies[0] = x_sends(0, 0)
    y_copies[0] = y_sends(0, 0)
    for step in range(NS):
        now = step % 2
        live = wide if step < DEGREE else nb

        @pl.loop(0, cx // 4)
        def _(i):
            shift_z(now, 4 * i + 1, 4, 0, cy)

        if step == DEGREE:
            def gram_plane(p, acc):
                f = [cur[fslot, b, p + 1, 0:cy, :] for b in range(nb)]
                return tuple(a + fold(f[i] * f[j]) for a, (i, j) in zip(acc, gram_pairs))

            grams = lax.fori_loop(
                0, cx, gram_plane, tuple(jnp.zeros((8, LANES), F32) for _ in gram_pairs)
            )

        for g, (first, last) in enumerate(parts(max(step, 1))):
            need = [y_copies[g]] if step > 0 else (y_copies if g == 0 else [])
            for copy in sum(need, []):
                copy.wait_recv()

            @pl.loop(first, last)
            def _(b):
                for p in range(1, cx + 1):
                    cur[now, b, p, cy : cy + 1, :] = yrecv[step, 0, b, p : p + 1, :]
                    cur[now, b, p, rows - 1 : rows, :] = yrecv[step, 1, b, p : p + 1, :]

            shift_z(now, 1, cx, cy, 8, first, last)

            @pl.loop(0, (min(last, live) - first) * (cx - 2))
            def _(t):
                apply_plane(step, first + t // (cx - 2), lax.rem(t, cx - 2) + 2)

        later_x, later_y = [], []
        for copy in y_copies[0] + y_copies[1] + x_copies[0][:2] + x_copies[1][:2]:
            copy.wait_send()
        for g, (first, last) in enumerate(parts(max(step, 1))):
            need = x_copies if step == 0 and g == 0 else ([] if step == 0 else [x_copies[g]])
            for copy in sum(need, []):
                copy.wait_recv()
            for b in range(first, last):
                source = g if step > 0 else (0 if b == nb else 1)
                for i, p in enumerate((cx + 1, 0)):
                    cur[now, b, p, 0:cy, :] = xrecv[step, i, b]
                    cur[now, b, p, cy : cy + 1, :] = crecv[step, source, i, 0, b : b + 1, :]
                    cur[now, b, p, rows - 1 : rows, :] = crecv[step, source, i, 1, b : b + 1, :]
            for p in (0, cx + 1):
                shift_z(now, p, 1, 0, rows, first, last)

            @pl.loop(first, min(last, live))
            def _(b):
                apply_plane(step, b, 1)
                apply_plane(step, b, cx)

            if step < DEGREE:
                later_x.append(x_sends(step + 1, g))
                later_y.append(y_sends(step + 1, g))
        for copy in x_copies[0][2:] + x_copies[1][2:]:
            copy.wait_send()
        x_copies, y_copies = later_x, later_y

    def dot_plane(p, acc):
        f = [cur[fslot, b, p + 1, 0:cy, :] for b in range(nb)]
        h = [cur[hslot, b, p + 1, 0:cy, :] for b in range(nb)]
        return tuple(a + fold(f[i] * h[j]) for a, (i, j) in zip(acc, pairs))

    dots = lax.fori_loop(0, cx, dot_plane, tuple(jnp.zeros((8, LANES), F32) for _ in pairs))
    everything = list(grams) + list(dots)
    slot = lax.broadcasted_iota(jnp.int32, (8, LANES), 0)
    quarter = lax.broadcasted_iota(jnp.int32, (8, LANES), 1) // 32
    payload = jnp.zeros((8, LANES), F32)
    for start in range(0, len(everything), 8):
        tile = jnp.zeros((8, LANES), F32)
        for k, part in enumerate(everything[start : start + 8]):
            tile = jnp.where(slot == k, jnp.sum(part, axis=0, keepdims=True), tile)
        tile = tile + pltpu.roll(tile, 64, 1)
        tile = tile + pltpu.roll(tile, 32, 1)
        payload = jnp.where(quarter == start // 8, tile, payload)

    def reduce_over(value, buffer, place, targets, send_sem, recv_sem):
        buffer[place] = value
        sends = []
        for k, target in enumerate(targets):
            sends.append(pltpu.make_async_remote_copy(
                src_ref=buffer.at[place], dst_ref=buffer.at[place],
                send_sem=send_sem.at[k], recv_sem=recv_sem.at[k],
                device_id=target, device_id_type=MESH,
            ))
        for copy in sends:
            copy.start()
        for copy in sends:
            copy.wait()
        total = buffer[0]
        for k in range(1, len(targets) + 1):
            total = total + buffer[k]
        return total

    value = reduce_over(payload, sum_x, gx, greeted[: nx - 1], ax_s, ax_r)
    value = reduce_over(
        value, sum_yz, gy * nz + gz, greeted[nx - 1 : nx - 1 + len(others)], ay_s, ay_r
    )
    value = value * (1.0 / (nx * ny * nz * cx * cy * cz))
    columns = [
        jnp.broadcast_to(
            jnp.sum(jnp.where(quarter == j, value, 0.0), axis=1, keepdims=True), (8, LANES)
        )
        for j in range((len(everything) + 7) // 8)
    ]

    def entry(k):
        return columns[k // 8][k % 8 : k % 8 + 1]

    gram = {pair: entry(k) for k, pair in enumerate(gram_pairs)}
    product = {pair: entry(k + len(gram_pairs)) for k, pair in enumerate(pairs)}
    low, recip = {}, []
    for q in range(nb):
        s = gram[q, q]
        for k in range(q):
            s = s - low[q, k] * low[q, k]
        recip.append(1.0 / jnp.sqrt(s))
        for p in range(q + 1, nb):
            s = gram[p, q]
            for k in range(q):
                s = s - low[p, k] * low[q, k]
            low[p, q] = s * recip[q]
    inv = {}
    for q in range(nb):
        inv[q, q] = recip[q]
        for p in range(q + 1, nb):
            s = low[p, q] * inv[q, q]
            for k in range(q + 1, p):
                s = s + low[p, k] * inv[k, q]
            inv[p, q] = -s * recip[p]

    @pl.loop(0, cx)
    def _(i):
        f = [cur[fslot, b, i + 1, 0:cy, :] for b in range(nb)]
        for p in range(nb):
            total = inv[p, 0] * f[0]
            for q in range(1, p + 1):
                total = total + inv[p, q] * f[q]
            basis_ref[p, i] = total

    left = {}
    for p in range(nb):
        for s in range(nb):
            total = inv[p, 0] * product[0, s]
            for r in range(1, p + 1):
                total = total + inv[p, r] * product[r, s]
            left[p, s] = total
    at_row = lax.broadcasted_iota(jnp.int32, (8, LANES), 0)
    at_lane = lax.broadcasted_iota(jnp.int32, (8, LANES), 1)
    ritz = jnp.zeros((8, LANES), F32)
    for p in range(nb):
        for q in range(nb):
            total = left[p, 0] * inv[q, 0]
            for s in range(1, q + 1):
                total = total + left[p, s] * inv[q, s]
            ritz = jnp.where((at_row == p) & (at_lane == q), total, ritz)
    ritz_ref[...] = ritz[0:nb, 0:nb]


def local(sizes, bands, stencil_coef):
    nx, ny, nz = sizes
    nb, cx, cy, cz = shape = bands.shape
    assert nz == 2 and cz == LANES and cy % 16 == 0 and nb == 4 and nx > 2 and cx % 4 == 0
    wide, rows, nyz = nb + 1, cy + 8, ny * nz
    up = -(-(cx + 2) // 8) * 8
    dma = pltpu.SemaphoreType.DMA
    return pl.pallas_call(
        functools.partial(kernel, sizes, shape),
        out_shape=(
            jax.ShapeDtypeStruct(shape, F32),
            jax.ShapeDtypeStruct((nb, nb), F32),
        ),
        in_specs=[
            pl.BlockSpec(memory_space=pltpu.HBM),
            pl.BlockSpec(memory_space=pltpu.SMEM),
        ],
        out_specs=(
            pl.BlockSpec(memory_space=pltpu.VMEM),
            pl.BlockSpec(memory_space=pltpu.VMEM),
        ),
        scratch_shapes=[
            pltpu.VMEM((2, wide, cx + 2, rows, LANES), F32),
            pltpu.VMEM((wide, cx + 2, rows, LANES), F32),
            pltpu.VMEM((wide, cx + 2, rows, LANES), F32),
            pltpu.VMEM((2, cy, LANES), F32),
            pltpu.VMEM((cx, cy // 2, LANES), F32),
            pltpu.VMEM((cx, cy // 2, LANES), F32),
            pltpu.VMEM((NS, 2, wide, cy, LANES), F32),
            pltpu.VMEM((NS, 2, wide, up, LANES), F32),
            pltpu.VMEM((NS, 2, wide, up, LANES), F32),
            pltpu.VMEM((NS, 2, 2, 2, 8, LANES), F32),
            pltpu.VMEM((NS, 2, 2, 2, 8, LANES), F32),
            pltpu.VMEM((nx, 8, LANES), F32),
            pltpu.VMEM((nyz, 8, LANES), F32),
            pltpu.VMEM((nb, 2 * LANES, 2 * LANES), jnp.bfloat16),
            pltpu.VMEM((9, 8, LANES), F32),
            dma, dma, dma,
            dma((NS, 2, 2)), dma((NS, 2, 2)),
            dma((NS, 2, 2)), dma((NS, 2, 2)),
            dma((NS, 2, 4)), dma((NS, 2, 4)),
            dma((nx - 1,)), dma((nx - 1,)),
            dma((nyz - 1,)), dma((nyz - 1,)),
        ],
        compiler_params=pltpu.CompilerParams(
            collective_id=0, has_side_effects=True, vmem_limit_bytes=40 * 1024 * 1024
        ),
    )(bands, stencil_coef)


def solution(mesh):
    placed = (P(None, "gx", "gy", "gz"), P())
    sizes = (mesh.shape["gx"], mesh.shape["gy"], mesh.shape["gz"])
    return jax.shard_map(
        functools.partial(local, sizes),
        mesh=mesh,
        in_specs=placed,
        out_specs=placed,
        check_vma=False,
    )
```

```python
import functools

import jax
import jax.numpy as jnp
from jax import lax
from jax.experimental import pallas as pl
from jax.experimental.pallas import tpu as pltpu
from jax.sharding import PartitionSpec as P

DEGREE = 4

lower_edge = 1.0
upper_edge = 6.5
HALF = (upper_edge - lower_edge) / 2
CENTER = (upper_edge + lower_edge) / 2

MESH = pl.DeviceIdType.MESH
NS = DEGREE + 1
LANES = 128
F32 = jnp.float32


def square(position, total):
    scaled = jnp.minimum(position, total - position).astype(F32) / (0.5 * total)
    return scaled * scaled


def kernel(
    sizes, shape, bands_ref, coef_ref, basis_ref, ritz_ref,
    cur, zm, zp, kin, packed, arrived, xrecv, ysend, yrecv, csend, crecv,
    sum_x, sum_yz, pick, edge_coef,
    load_sem, zs_sem, zr_sem, xs_sem, xr_sem, ys_sem, yr_sem, cs_sem, cr_sem,
    ax_s, ax_r, ay_s, ay_r,
):
    nx, ny, nz = sizes
    nb, cx, cy, cz = shape
    rows = cy + 8
    wide = nb + 1
    gx, gy, gz = lax.axis_index("gx"), lax.axis_index("gy"), lax.axis_index("gz")

    def dev(dx, dy, dz):
        return (lax.rem(gx + dx + nx, nx), lax.rem(gy + dy + ny, ny), lax.rem(gz + dz + nz, nz))

    load = pltpu.make_async_copy(bands_ref, cur.at[0, 0:nb, 1 : cx + 1, 0:cy], load_sem)
    load.start()

    barrier = pltpu.get_barrier_semaphore()
    greeted = [dev(k, 0, 0) for k in range(1, nx)]
    others = [(j, k) for j in range(ny) for k in range(nz) if (j, k) != (0, 0)]
    greeted += [dev(0, j, k) for j, k in others]
    greeted += [dev(dx, dy, 0) for dx in (-1, 1) for dy in (-1, 1)]
    for target in greeted:
        pl.semaphore_signal(barrier, inc=1, device_id=target, device_id_type=MESH)

    lane = lax.broadcasted_iota(jnp.int32, (cy, LANES), 1)
    row = lax.broadcasted_iota(jnp.int32, (cy, LANES), 0)
    group = lax.rem(lane, 32)
    fy = square(row + gy * cy, ny * cy)
    kin[0] = fy + square(lane + gz * cz, nz * cz)
    strip_z = gz * cz + jnp.where(group < 16, group - 8, group + (cz - 24)) + nz * cz
    kin[1] = fy + square(lax.rem(strip_z, nz * cz), nz * cz)

    take = lax.broadcasted_iota(jnp.int32, (2 * LANES, 2 * LANES), 0)
    give = lax.broadcasted_iota(jnp.int32, (2 * LANES, 2 * LANES), 1)
    inside = ((give < LANES) & (take == give - 1)) | (
        (give >= LANES) & (take < LANES) & (take == give - LANES + 1)
    )
    for b in range(nb):
        before = (give == 0) & (take == LANES + 32 * b + 7)
        after = (give == 2 * LANES - 1) & (take == LANES + 32 * b + 24)
        pick[b] = jnp.where(inside | before | after, 1.0, 0.0).astype(jnp.bfloat16)

    tile_row = lax.broadcasted_iota(jnp.int32, (8, LANES), 0)
    for x in range(3):
        for z in range(3):
            edge_coef[3 * x + z] = jnp.where(
                tile_row < 4, coef_ref[9 * x + 6 + z], coef_ref[9 * x + z]
            )

    load.wait()

    half_rows = cy // 2

    def pick_strip(plane):
        result = jnp.zeros((cy, LANES), F32)
        for b in range(nb):
            v = cur[0, b, plane, 0:cy, :]
            left = pltpu.roll(v, (32 * b + 8) % LANES, 1)
            right = pltpu.roll(v, (32 * b + 24) % LANES, 1)
            mine = jnp.where(group < 16, left, right)
            result = jnp.where(lane // 32 == b, mine, result)
        return result

    outer = (group < 8) | (group >= 24)
    outer_half = outer[0:half_rows]

    @pl.loop(0, cx)
    def _(i):
        own = pick_strip(i + 1)
        cur[0, nb, i + 1, 0:cy, :] = own
        packed[i] = jnp.where(
            outer_half, own[0:half_rows], pltpu.roll(own[half_rows:cy], 16, 1)
        )

    pl.semaphore_wait(barrier, len(greeted))

    def parts(step):
        return ((nb, wide), (0, nb)) if step == 0 else ((2, wide), (0, 2))

    def x_sends(step, g):
        now = step % 2
        first, last = parts(step)[g]
        copies = []
        for i, p in enumerate((1, cx)):
            copies.append(pltpu.make_async_remote_copy(
                src_ref=cur.at[now, first:last, p, 0:cy], dst_ref=xrecv.at[step, i, first:last],
                send_sem=xs_sem.at[step, g, i], recv_sem=xr_sem.at[step, g, i],
                device_id=dev(2 * i - 1, 0, 0), device_id_type=MESH,
            ))
            copies[-1].start()
        for i, p in enumerate((1, cx)):
            for j, r in enumerate((0, cy - 1)):
                for b in range(first, last):
                    csend[step, g, i, j, b : b + 1, :] = cur[now, b, p, r : r + 1, :]
                copies.append(pltpu.make_async_remote_copy(
                    src_ref=csend.at[step, g, i, j], dst_ref=crecv.at[step, g, i, j],
                    send_sem=cs_sem.at[step, g, 2 * i + j], recv_sem=cr_sem.at[step, g, 2 * i + j],
                    device_id=dev(2 * i - 1, 2 * j - 1, 0), device_id_type=MESH,
                ))
                copies[-1].start()
        return copies

    def y_sends(step, g):
        now = step % 2
        first, last = parts(step)[g]
        copies = []

        @pl.loop(first, last)
        def _(b):
            for p in range(1, cx + 1):
                ysend[step, 0, b, p : p + 1, :] = cur[now, b, p, 0:1, :]
                ysend[step, 1, b, p : p + 1, :] = cur[now, b, p, cy - 1 : cy, :]

        for j in range(2):
            copies.append(pltpu.make_async_remote_copy(
                src_ref=ysend.at[step, j, first:last], dst_ref=yrecv.at[step, j, first:last],
                send_sem=ys_sem.at[step, g, j], recv_sem=yr_sem.at[step, g, j],
                device_id=dev(0, 2 * j - 1, 0), device_id_type=MESH,
            ))
            copies[-1].start()
        return copies

    z_copy = pltpu.make_async_remote_copy(
        src_ref=packed, dst_ref=arrived, send_sem=zs_sem, recv_sem=zr_sem,
        device_id=dev(0, 0, 1), device_id_type=MESH,
    )
    z_copy.start()
    x_copies = [None, x_sends(0, 1)]
    y_copies = [None, y_sends(0, 1)]
    z_copy.wait()

    @pl.loop(0, cx)
    def _(i):
        there = arrived[i]
        own = cur[0, nb, i + 1, 0:cy, :]
        full = jnp.concatenate([there, pltpu.roll(there, LANES - 16, 1)], axis=0)
        cur[0, nb, i + 1, 0:cy, :] = jnp.where(outer, full, own)

    def halves(v):
        high = v.astype(jnp.bfloat16)
        low = (v - high.astype(F32)).astype(jnp.bfloat16)
        return jnp.concatenate([high, low], axis=0)

    def shift_z(now, plane, planes, first, count, band=0, end=None):
        part, which = pl.ds(first, count), pl.ds(plane, planes)
        m = planes * count
        strip = cur[now, nb, which, part, :].reshape(m, LANES)
        end = wide if end is None else end
        if end == wide:
            zm[nb, which, part, :] = pltpu.roll(strip, 1, 1).reshape(planes, count, LANES)
            zp[nb, which, part, :] = pltpu.roll(strip, LANES - 1, 1).reshape(planes, count, LANES)
        strip = halves(strip)
        for b in range(band, min(end, nb)):
            v = halves(cur[now, b, which, part, :].reshape(m, LANES))
            moved = jnp.dot(
                jnp.concatenate([v, strip], axis=1), pick[b], preferred_element_type=F32
            )
            moved = moved[0:m] + moved[m : 2 * m]
            zm[b, which, part, :] = moved[:, 0:LANES].reshape(planes, count, LANES)
            zp[b, which, part, :] = moved[:, LANES:].reshape(planes, count, LANES)

    def apply_plane(step, b, plane):
        now, later = step % 2, 1 - step % 2
        fields = (zm, cur.at[now], zp)
        sums = []
        for y in range(3):
            total = None
            for x in range(3):
                for z in range(3):
                    c = coef_ref[9 * x + 3 * y + z]
                    term = c * fields[z][b, plane + (x - 1), 0:cy, :]
                    total = term if total is None else total + term
            sums.append(total)
        edge = None
        for x in range(3):
            for z in range(3):
                term = edge_coef[3 * x + z] * fields[z][b, plane + (x - 1), cy:rows, :]
                edge = term if edge is None else edge + term
        sums[0] = jnp.concatenate([sums[0], edge], axis=0)
        sums[2] = jnp.concatenate([sums[2], edge], axis=0)
        v = cur[now, b, plane, 0:cy, :]
        scale = 1.0 / HALF if step == 0 else (2.0 / HALF if step < DEGREE else 1.0)
        fx = square(gx * cx + plane - 1, nx * cx)
        if step < DEGREE:
            fx = fx - CENTER
        total = sums[1] + pltpu.roll(sums[0], 1, 0)[0:cy] + pltpu.roll(sums[2], rows - 1, 0)[0:cy]
        total = (total + (kin[b // nb] + fx) * v) * scale
        if 0 < step < DEGREE:
            total = total - cur[later, b, plane, 0:cy, :]
        cur[later, b, plane, 0:cy, :] = total

    gram_pairs = [(p, q) for p in range(nb) for q in range(p + 1)]
    pairs = [(p, q) for p in range(nb) for q in range(nb)]
    fslot, hslot = DEGREE % 2, 1 - DEGREE % 2

    def fold(a):
        total = a[0:8]
        for k in range(8, cy, 8):
            total = total + a[k : k + 8]
        return total

    x_copies[0] = x_sends(0, 0)
    y_copies[0] = y_sends(0, 0)
    for step in range(NS):
        now = step % 2
        live = wide if step < DEGREE else nb

        @pl.loop(0, cx // 4)
        def _(i):
            shift_z(now, 4 * i + 1, 4, 0, cy)

        if step == DEGREE:
            def gram_plane(p, acc):
                f = [cur[fslot, b, p + 1, 0:cy, :] for b in range(nb)]
                return tuple(a + fold(f[i] * f[j]) for a, (i, j) in zip(acc, gram_pairs))

            grams = lax.fori_loop(
                0, cx, gram_plane, tuple(jnp.zeros((8, LANES), F32) for _ in gram_pairs)
            )

        for g, (first, last) in enumerate(parts(max(step, 1))):
            need = [y_copies[g]] if step > 0 else (y_copies if g == 0 else [])
            for copy in sum(need, []):
                copy.wait_recv()

            @pl.loop(first, last)
            def _(b):
                for p in range(1, cx + 1):
                    cur[now, b, p, cy : cy + 1, :] = yrecv[step, 0, b, p : p + 1, :]
                    cur[now, b, p, rows - 1 : rows, :] = yrecv[step, 1, b, p : p + 1, :]

            shift_z(now, 1, cx, cy, 8, first, last)

            @pl.loop(0, (min(last, live) - first) * (cx - 2))
            def _(t):
                apply_plane(step, first + t // (cx - 2), lax.rem(t, cx - 2) + 2)

        later_x, later_y = [], []
        for copy in y_copies[0] + y_copies[1] + x_copies[0][:2] + x_copies[1][:2]:
            copy.wait_send()
        for g, (first, last) in enumerate(parts(max(step, 1))):
            need = x_copies if step == 0 and g == 0 else ([] if step == 0 else [x_copies[g]])
            for copy in sum(need, []):
                copy.wait_recv()
            for b in range(first, last):
                source = g if step > 0 else (0 if b == nb else 1)
                for i, p in enumerate((cx + 1, 0)):
                    cur[now, b, p, 0:cy, :] = xrecv[step, i, b]
                    cur[now, b, p, cy : cy + 1, :] = crecv[step, source, i, 0, b : b + 1, :]
                    cur[now, b, p, rows - 1 : rows, :] = crecv[step, source, i, 1, b : b + 1, :]
            for p in (0, cx + 1):
                shift_z(now, p, 1, 0, rows, first, last)

            @pl.loop(first, min(last, live))
            def _(b):
                apply_plane(step, b, 1)
                apply_plane(step, b, cx)

            if step < DEGREE:
                later_x.append(x_sends(step + 1, g))
                later_y.append(y_sends(step + 1, g))
        for copy in x_copies[0][2:] + x_copies[1][2:]:
            copy.wait_send()
        x_copies, y_copies = later_x, later_y

    def dot_plane(p, acc):
        f = [cur[fslot, b, p + 1, 0:cy, :] for b in range(nb)]
        h = [cur[hslot, b, p + 1, 0:cy, :] for b in range(nb)]
        return tuple(a + fold(f[i] * h[j]) for a, (i, j) in zip(acc, pairs))

    dots = lax.fori_loop(0, cx, dot_plane, tuple(jnp.zeros((8, LANES), F32) for _ in pairs))
    everything = list(grams) + list(dots)
    slot = lax.broadcasted_iota(jnp.int32, (8, LANES), 0)
    quarter = lax.broadcasted_iota(jnp.int32, (8, LANES), 1) // 32
    payload = jnp.zeros((8, LANES), F32)
    for start in range(0, len(everything), 8):
        tile = jnp.zeros((8, LANES), F32)
        for k, part in enumerate(everything[start : start + 8]):
            tile = jnp.where(slot == k, jnp.sum(part, axis=0, keepdims=True), tile)
        tile = tile + pltpu.roll(tile, 64, 1)
        tile = tile + pltpu.roll(tile, 32, 1)
        payload = jnp.where(quarter == start // 8, tile, payload)

    def reduce_over(value, buffer, place, targets, send_sem, recv_sem):
        buffer[place] = value
        sends = []
        for k, target in enumerate(targets):
            sends.append(pltpu.make_async_remote_copy(
                src_ref=buffer.at[place], dst_ref=buffer.at[place],
                send_sem=send_sem.at[k], recv_sem=recv_sem.at[k],
                device_id=target, device_id_type=MESH,
            ))
        for copy in sends:
            copy.start()
        for copy in sends:
            copy.wait()
        total = buffer[0]
        for k in range(1, len(targets) + 1):
            total = total + buffer[k]
        return total

    value = reduce_over(payload, sum_x, gx, greeted[: nx - 1], ax_s, ax_r)
    value = reduce_over(
        value, sum_yz, gy * nz + gz, greeted[nx - 1 : nx - 1 + len(others)], ay_s, ay_r
    )
    value = value * (1.0 / (nx * ny * nz * cx * cy * cz))
    columns = [
        jnp.broadcast_to(
            jnp.sum(jnp.where(quarter == j, value, 0.0), axis=1, keepdims=True), (8, LANES)
        )
        for j in range((len(everything) + 7) // 8)
    ]

    def entry(k):
        return columns[k // 8][k % 8 : k % 8 + 1]

    gram = {pair: entry(k) for k, pair in enumerate(gram_pairs)}
    product = {pair: entry(k + len(gram_pairs)) for k, pair in enumerate(pairs)}
    low, recip = {}, []
    for q in range(nb):
        s = gram[q, q]
        for k in range(q):
            s = s - low[q, k] * low[q, k]
        recip.append(1.0 / jnp.sqrt(s))
        for p in range(q + 1, nb):
            s = gram[p, q]
            for k in range(q):
                s = s - low[p, k] * low[q, k]
            low[p, q] = s * recip[q]
    inv = {}
    for q in range(nb):
        inv[q, q] = recip[q]
        for p in range(q + 1, nb):
            s = low[p, q] * inv[q, q]
            for k in range(q + 1, p):
                s = s + low[p, k] * inv[k, q]
            inv[p, q] = -s * recip[p]

    @pl.loop(0, cx)
    def _(i):
        f = [cur[fslot, b, i + 1, 0:cy, :] for b in range(nb)]
        for p in range(nb):
            total = inv[p, 0] * f[0]
            for q in range(1, p + 1):
                total = total + inv[p, q] * f[q]
            basis_ref[p, i] = total

    left = {}
    for p in range(nb):
        for s in range(nb):
            total = inv[p, 0] * product[0, s]
            for r in range(1, p + 1):
                total = total + inv[p, r] * product[r, s]
            left[p, s] = total
    at_row = lax.broadcasted_iota(jnp.int32, (8, LANES), 0)
    at_lane = lax.broadcasted_iota(jnp.int32, (8, LANES), 1)
    ritz = jnp.zeros((8, LANES), F32)
    for p in range(nb):
        for q in range(nb):
            total = left[p, 0] * inv[q, 0]
            for s in range(1, q + 1):
                total = total + left[p, s] * inv[q, s]
            ritz = jnp.where((at_row == p) & (at_lane == q), total, ritz)
    ritz_ref[...] = ritz[0:nb, 0:nb]


def local(sizes, bands, stencil_coef):
    nx, ny, nz = sizes
    nb, cx, cy, cz = shape = bands.shape
    assert nz == 2 and cz == LANES and cy % 16 == 0 and nb == 4 and nx > 2 and cx % 4 == 0
    wide, rows, nyz = nb + 1, cy + 8, ny * nz
    up = -(-(cx + 2) // 8) * 8
    dma = pltpu.SemaphoreType.DMA
    return pl.pallas_call(
        functools.partial(kernel, sizes, shape),
        out_shape=(
            jax.ShapeDtypeStruct(shape, F32),
            jax.ShapeDtypeStruct((nb, nb), F32),
        ),
        in_specs=[
            pl.BlockSpec(memory_space=pltpu.HBM),
            pl.BlockSpec(memory_space=pltpu.SMEM),
        ],
        out_specs=(
            pl.BlockSpec(memory_space=pltpu.VMEM),
            pl.BlockSpec(memory_space=pltpu.VMEM),
        ),
        scratch_shapes=[
            pltpu.VMEM((2, wide, cx + 2, rows, LANES), F32),
            pltpu.VMEM((wide, cx + 2, rows, LANES), F32),
            pltpu.VMEM((wide, cx + 2, rows, LANES), F32),
            pltpu.VMEM((2, cy, LANES), F32),
            pltpu.VMEM((cx, cy // 2, LANES), F32),
            pltpu.VMEM((cx, cy // 2, LANES), F32),
            pltpu.VMEM((NS, 2, wide, cy, LANES), F32),
            pltpu.VMEM((NS, 2, wide, up, LANES), F32),
            pltpu.VMEM((NS, 2, wide, up, LANES), F32),
            pltpu.VMEM((NS, 2, 2, 2, 8, LANES), F32),
            pltpu.VMEM((NS, 2, 2, 2, 8, LANES), F32),
            pltpu.VMEM((nx, 8, LANES), F32),
            pltpu.VMEM((nyz, 8, LANES), F32),
            pltpu.VMEM((nb, 2 * LANES, 2 * LANES), jnp.bfloat16),
            pltpu.VMEM((9, 8, LANES), F32),
            dma, dma, dma,
            dma((NS, 2, 2)), dma((NS, 2, 2)),
            dma((NS, 2, 2)), dma((NS, 2, 2)),
            dma((NS, 2, 4)), dma((NS, 2, 4)),
            dma((nx - 1,)), dma((nx - 1,)),
            dma((nyz - 1,)), dma((nyz - 1,)),
        ],
        compiler_params=pltpu.CompilerParams(
            collective_id=0, has_side_effects=True, vmem_limit_bytes=60 * 1024 * 1024
        ),
    )(bands, stencil_coef)


def solution(mesh):
    placed = (P(None, "gx", "gy", "gz"), P())
    sizes = (mesh.shape["gx"], mesh.shape["gy"], mesh.shape["gz"])
    return jax.shard_map(
        functools.partial(local, sizes),
        mesh=mesh,
        in_specs=placed,
        out_specs=placed,
        check_vma=False,
    )
```
